256 devices in a mesh: band: 2 (over z_hi), space: 128 (over z_lo, x, y, core).
Axes of the slice: x: 4, y: 4, z: 8 (z_hi: 2, z_lo: 4; z = z_hi * 4 + z_lo), core: 2. Of those that a mesh axis runs over, the one named last changes fastest.
Arguments:
- psi: float32 [32, 128, 8, 8, 128], P('band', 'space'), may hold values from -12 to 12
- potential: float32 [128, 8, 8, 128], P('space'), may hold values from -3 to 0
- projector: float32 [128, 32, 16, 128], P('space'), may hold values from -0.5 to 0.5
- coupling: float32 [128, 32, 16], P('space'), may hold values from 0.5 to 4
- slot_live: int32 [128], P('space'), may hold values from 0 to 32, as said below
- point_count: int32 [128, 32], P('space'), may hold values from 64 to 128, as said below
- point_index: int32 [128, 32, 128], P('space'), may hold values from 0 to 8191, as said below
Outputs:
- filtered: float32 [32, 128, 8, 8, 128], P('band', 'space')
- gram: float32 [32, 32], P('band')
The draws below stay inside these ranges and needn't reach their ends.
Inputs may be any that keep to these rules, and one draw needn't show every extreme that they name: `slot_live`: tiles 128 // 2 and above (the vacuum half along the first grid dimension) own no atoms; some tile owns exactly 32. `point_count`: slot 0 of every tile uses all 128 points. `point_index`: cells of the slot's own tile near an atom centre; cells may repeat.
All inputs are finite; a program needn't handle non-finite values.
Results may differ from the reference program's by a relative error of at most 0.0001.
Values sent between devices are 32-bit elements; how exact they have to be, the bound alone decides.
A program may use at most 192 MiB of HBM per device.

```python
import math
import jax
import jax.numpy as jnp
from jax import lax

BANDS = 32
NPROJ = 16
PTS = 128
DEGREE = 2
CX = 8
CY = 8
CZ = 128
ASLOT = 32
TILES = 128


def draw_slot_live(key, part):
    key = jax.random.fold_in(key, 11)
    live = jax.random.randint(key, (TILES,), ASLOT // 4, ASLOT + 1)
    tiles = jnp.arange(TILES, dtype=jnp.int32)
    live = jnp.where(tiles == 0, ASLOT, live)
    return jnp.where(tiles < TILES // 2, live, 0).astype(jnp.int32)


def draw_point_count(key, part):
    key = jax.random.fold_in(key, 12)
    counts = jax.random.randint(key, (TILES, ASLOT), PTS // 2, PTS + 1)
    slots = jnp.arange(ASLOT, dtype=jnp.int32)[None, :]
    return jnp.where(slots == 0, PTS, counts).astype(jnp.int32)


def draw_point_index(key, part):
    key = jax.random.fold_in(key, 13)
    keys = jax.random.split(key, 6)
    centre_x = jax.random.randint(keys[0], (TILES, ASLOT, 1), 0, CX)
    centre_y = jax.random.randint(keys[1], (TILES, ASLOT, 1), 0, CY)
    centre_z = jax.random.randint(keys[2], (TILES, ASLOT, 1), 0, CZ)
    step_x = jax.random.randint(keys[3], (TILES, ASLOT, PTS), -2, 3)
    step_y = jax.random.randint(keys[4], (TILES, ASLOT, PTS), -2, 3)
    step_z = jax.random.randint(keys[5], (TILES, ASLOT, PTS), -3, 4)
    cell_x = (centre_x + step_x) % CX
    cell_y = (centre_y + step_y) % CY
    cell_z = (centre_z + step_z) % CZ
    flat = (cell_x * CY + cell_y) * CZ + cell_z
    slots = jnp.arange(ASLOT, dtype=jnp.int32)[None, :, None]
    points = jnp.arange(PTS, dtype=jnp.int32)[None, None, :]
    flat = jnp.where((slots == 0) & (points == 0), CX * CY * CZ - 1, flat)
    flat = jnp.where((slots == 1) & (points == 0), 0, flat)
    return flat.astype(jnp.int32)


def levels(key, extent, cuts, least, largest):
    gain, own = 1.0, jax.random.fold_in(key, 6)
    for dim, shards_of in cuts:
        draws = jnp.exp(jax.random.uniform(jax.random.fold_in(own, dim), (shards_of,), jnp.float32, least / len(cuts), largest / len(cuts)))
        gain = gain * jnp.repeat(draws, extent[dim] // shards_of).reshape([-1 if axis == dim else 1 for axis in range(len(extent))])
    return gain


def gaussian(key, dims, scale, most, pieces=(), held_as=jnp.bfloat16):
    entries = jax.random.normal(key, dims, jnp.float32) * scale
    if len(pieces) > 0:
        entries = levels(key, dims, pieces, -0.22, 0.18) * entries
    return jnp.clip(entries, min=-most, max=most).astype(held_as)


def setup_inputs(seed: int = 0) -> dict:
    splits = jax.random.split(jax.random.key(seed), 8)
    psi = gaussian(splits[0], (BANDS, TILES, CX, CY, CZ), 2.0, 12.0, ((0, 2), (1, 128)), jnp.float32)
    potential = jnp.clip(-3.0 + 3.0 * jax.random.uniform(splits[1], (TILES, CX, CY, CZ), jnp.float32) ** levels(splits[1], (TILES, CX, CY, CZ), ((0, 128),), -0.2, 0.2), -3.0, 0.0)
    projector = gaussian(splits[2], (TILES, ASLOT, NPROJ, PTS), PTS ** -0.5, 0.5, ((0, 128),), jnp.float32)
    coupling = jnp.clip(jnp.exp(math.log(4.0) - 2.0794415 * jax.random.uniform(splits[3], (TILES, ASLOT, NPROJ), jnp.float32) ** levels(splits[3], (TILES, ASLOT, NPROJ), ((0, 128),), -0.2, 0.2)), 0.5, 4.0)
    slot_live = draw_slot_live(jax.random.fold_in(splits[7], 71), 0)
    point_count = draw_point_count(jax.random.fold_in(splits[7], 71), 0)
    point_index = draw_point_index(jax.random.fold_in(splits[7], 71), 0)
    return dict(psi=psi, potential=potential, projector=projector, coupling=coupling, slot_live=slot_live, point_count=point_count, point_index=point_index)


LAP_COEFFS = (-5369.0 / 1800.0, 12.0 / 7.0, -15.0 / 56.0, 10.0 / 189.0, -1.0 / 112.0, 2.0 / 1925.0, -1.0 / 16632.0)
KINETIC = -2.0
FILTERS = ((10.0, 60.0, -2.0), (6.0, 60.0, -2.0))


def projector_weights(projector, point_count, slot_live):
    points = lax.broadcasted_iota(jnp.int32, projector.shape, projector.ndim - 1)
    slots = lax.broadcasted_iota(jnp.int32, projector.shape, projector.ndim - 3)
    keep = (points < point_count[..., None, None]) & (slots < slot_live[..., None, None, None])
    return jnp.where(keep, projector, jnp.zeros_like(projector))


def to_global(field):
    rows = field.shape[0] // 2
    return field.reshape(rows, 2, CX, CY, CZ).transpose(0, 2, 1, 3, 4).reshape(rows * CX, 2 * CY, CZ)


def to_tiles(grid):
    rows = grid.shape[0] // CX
    return grid.reshape(rows, CX, 2, CY, CZ).transpose(0, 2, 1, 3, 4).reshape(rows * 2, CX, CY, CZ)


def hamiltonian(field, potential, weights, coupling, flat_index):
    grid = to_global(field)
    lap = 3.0 * LAP_COEFFS[0] * grid
    for shift in range(1, 7):
        total = jnp.zeros_like(grid)
        for axis_no in range(3):
            total = total + jnp.roll(grid, shift, axis_no) + jnp.roll(grid, -shift, axis_no)
        lap = lap + LAP_COEFFS[shift] * total
    flat = field.reshape(TILES, -1)
    values = jnp.take_along_axis(flat, flat_index, axis=1).reshape(TILES, ASLOT, PTS)
    coef = jnp.einsum('tsjp,tsp->tsj', weights, values, precision=lax.Precision.HIGHEST)
    scaled = coef * coupling
    contrib = jnp.einsum('tsjp,tsj->tsp', weights, scaled, precision=lax.Precision.HIGHEST)
    tile_rows = jnp.broadcast_to(jnp.arange(TILES, dtype=jnp.int32)[:, None], flat_index.shape)
    added = jnp.zeros_like(flat).at[tile_rows, flat_index].add(contrib.reshape(TILES, -1))
    return to_tiles(KINETIC * lap) + potential * field + added.reshape(field.shape)


def filter_pass(block, cuts, apply_ham):
    low, high, bottom = cuts
    half = (high - low) / 2.0
    centre = (high + low) / 2.0
    sigma = half / (bottom - centre)
    tau = 2.0 / sigma
    older = block
    newer = (apply_ham(block) - centre * block) * (sigma / half)
    for step in range(DEGREE - 1):
        sigma_next = 1.0 / (tau - sigma)
        following = (apply_ham(newer) - centre * newer) * (2.0 * sigma_next / half) - (sigma * sigma_next) * older
        older, newer, sigma = newer, following, sigma_next
    return newer


def reference(psi, potential, projector, coupling, slot_live, point_count, point_index):
    weights = projector_weights(projector, point_count, slot_live)
    flat_index = point_index.reshape(TILES, -1).astype(jnp.int32)

    def apply_ham(field):
        return hamiltonian(field, potential, weights, coupling, flat_index)

    def one_band(field):
        first = filter_pass(field, FILTERS[0], apply_ham)
        return filter_pass(first, FILTERS[1], apply_ham)

    filtered = lax.map(one_band, psi)
    flat_out = filtered.reshape(BANDS, -1)
    gram = jnp.dot(flat_out, flat_out.T, precision=lax.Precision.HIGHEST, preferred_element_type=jnp.float32)
    gram = gram / flat_out.shape[1]
    return filtered, gram
```

```python
import functools

import jax
import jax.numpy as jnp
from jax import lax
from jax.experimental import pallas as pl
from jax.experimental.pallas import tpu as pltpu
from jax.sharding import PartitionSpec as P

LAP_COEFFS = (
    -5369.0 / 1800.0,
    12.0 / 7.0,
    -15.0 / 56.0,
    10.0 / 189.0,
    -1.0 / 112.0,
    2.0 / 1925.0,
    -1.0 / 16632.0,
)
KINETIC = -2.0
FILTERS = ((10.0, 60.0, -2.0), (6.0, 60.0, -2.0))
WIDTH = 6
MESH = pl.DeviceIdType.MESH
F32, BF16 = jnp.float32, jnp.bfloat16

SX, SY, SZ = 8, 8, 128
ROWS = SX * SY
GB = 8
PAIRS = ROWS // 2
SLOTS, NPROJ, PTS = 32, 16, 128
POINTS = SLOTS * PTS
CHUNK = 1024
CHUNK_SLOTS = CHUNK // PTS
STEPS = 4


def step_constants():
    scale, carry, shift = [], [], []
    for low, high, bottom in FILTERS:
        half = (high - low) / 2.0
        centre = (high + low) / 2.0
        sigma = half / (bottom - centre)
        tau = 2.0 / sigma
        following = 1.0 / (tau - sigma)
        scale += [sigma / half, 2.0 * following / half]
        carry += [0.0, -sigma * following]
        shift += [centre, centre]
    return scale, carry, shift


SCALE, CARRY, SHIFT = step_constants()


def chosen(step, values):
    out = jnp.float32(values[-1])
    for at in range(len(values) - 2, -1, -1):
        out = jnp.where(step == at, jnp.float32(values[at]), out)
    return out


def two_parts(value):
    high = value.astype(BF16).astype(F32)
    return jnp.concatenate([high, value - high], axis=0).astype(BF16)


def dot(a, b):
    return jnp.dot(a, b, preferred_element_type=F32)


def dot_t(a, b):
    return lax.dot_general(a, b, (((1,), (1,)), ((), ())), preferred_element_type=F32)


def kernel(
    tiles,
    psi_in,
    pot_in,
    projector_in,
    coupling_in,
    slot_live_in,
    point_count_in,
    point_index_in,
    out,
    gram,
    ready,
    psi,
    pot,
    projector,
    coupling,
    slot_live,
    point_count,
    point_index,
    field,
    low_x,
    high_x,
    other_y,
    other_band,
    hot,
    pair_of,
    pair_of16,
    operator,
    parts,
    added,
    local,
    wide,
    wide_other,
    send,
    recv,
    send_band,
    recv_band,
    sums,
    sums_in,
    send_sums,
    recv_sums,
    load,
):
    groups = field.shape[1]
    band = lax.axis_index("band")
    tile = lax.axis_index("space")
    up = (band, lax.rem(tile + 2, tiles))
    down = (band, lax.rem(tile + tiles - 2, tiles))
    beside = (band, tile + 1 - 2 * lax.rem(tile, 2))
    across = (1 - band, tile)

    def turned_by(span, low, away):
        return (band, tile - lax.rem(tile, span) + lax.rem(lax.rem(tile, span) + away * low, span))

    depth = tiles // 32
    ring = band * depth + tile // 32

    def along(away):
        place = lax.rem(ring + away, 2 * depth)
        return (place // depth, lax.rem(place, depth) * 32 + lax.rem(tile, 32))

    phases = (
        [beside],
        [turned_by(8, 2, away) for away in range(1, 4)],
        [turned_by(32, 8, away) for away in range(1, 4)],
        [along(away) for away in range(1, 2 * depth)],
    )

    barrier = pltpu.get_barrier_semaphore()
    greeted = [up, down] + [device for phase in phases for device in phase]
    for device in greeted:
        pl.semaphore_signal(barrier, inc=1, device_id=device, device_id_type=MESH)

    def loaded(src, dst, at):
        return pltpu.make_async_copy(src, dst, load.at[at])

    loads = [
        loaded(psi_in.at[pl.ds(g * GB, GB)], psi.at[pl.ds(g * GB, GB)], g) for g in range(groups)
    ] + [
        loaded(src, dst, groups + at)
        for at, (src, dst) in enumerate(
            (
                (point_index_in, point_index),
                (projector_in, projector),
                (coupling_in, coupling),
                (slot_live_in, slot_live),
                (point_count_in, point_count),
                (pot_in, pot),
            )
        )
    ]
    for copy in loads:
        copy.start()

    def halo_copies(turn, g):
        def copy(src, dst, which, device):
            return pltpu.make_async_remote_copy(
                src_ref=src,
                dst_ref=dst,
                send_sem=send.at[turn, g, which],
                recv_sem=recv.at[turn, g, which],
                device_id=device,
                device_id_type=MESH,
            )

        edge = WIDTH * SY
        return (
            copy(field.at[turn, g, pl.ds(ROWS - edge, edge)], low_x.at[turn, g], 0, up),
            copy(field.at[turn, g, pl.ds(0, edge)], high_x.at[turn, g], 1, down),
            copy(field.at[turn, g], other_y.at[turn, g], 2, beside),
        )

    def band_copy(g):
        return pltpu.make_async_remote_copy(
            src_ref=field.at[0, g, pl.ds(band * (ROWS // 2), ROWS // 2)],
            dst_ref=other_band.at[g],
            send_sem=send_band.at[g],
            recv_sem=recv_band.at[g],
            device_id=across,
            device_id_type=MESH,
        )

    def split_pair(pair, first, second):
        parts[pair] = two_parts(jnp.concatenate([first, second], axis=1))

    for g in range(groups):
        loads[g].wait()
        for b in range(GB):
            for x in range(SX):
                field[0, g, pl.ds(x * SY, SY), b, :] = psi[g * GB + b, pl.ds(x * SY, SY)]
        if g == 0:
            pl.semaphore_wait(barrier, len(greeted))
        for copy in halo_copies(0, g):
            copy.start()

    field[1] = jnp.zeros(field.shape[1:], F32)
    for copy in loads[groups:]:
        copy.wait()

    @pl.loop(0, SLOTS, unroll=4)
    def _(s):
        cols = pl.ds(pl.multiple_of(s * PTS, PTS), PTS)
        index = point_index[pl.ds(s, 1), :]
        place = jnp.broadcast_to(index & 255, (256, PTS))
        spots = lax.broadcasted_iota(jnp.int32, (256, PTS), 0)
        hot[:, cols] = jnp.where(place == spots, 1.0, 0.0).astype(BF16)
        pair = jnp.broadcast_to(index >> 8, (16, PTS))
        pair_of[:, cols] = pair
        pair_of16[:, cols] = pair.astype(F32).astype(BF16)
        points = lax.broadcasted_iota(jnp.int32, (NPROJ, PTS), 1)
        slots = jnp.full((NPROJ, PTS), s, jnp.int32)
        keep = (points < point_count[s]) & (slots < slot_live[0])
        weights = jnp.where(keep, projector[s], 0.0)
        mine = lax.broadcasted_iota(jnp.int32, (NPROJ, SLOTS), 1) == s
        couple = jnp.sum(jnp.where(mine, coupling[...], 0.0), axis=1, keepdims=True)
        coupled = weights * couple
        weights_high = weights.astype(BF16).astype(F32)
        coupled_high = coupled.astype(BF16).astype(F32)
        left = jnp.concatenate([weights_high, weights_high, weights - weights_high], axis=0)
        right = jnp.concatenate([coupled_high, coupled - coupled_high, coupled_high], axis=0)
        square = dot(left.T.astype(BF16), right.astype(BF16))
        square_high = square.astype(BF16).astype(F32)
        operator[s] = jnp.concatenate([square_high, square - square_high], axis=1).astype(BF16)

    def nonlocal_chunk(g, c):
        cols = pl.ds(c * CHUNK, CHUNK)
        one_hot = hot[:, cols]
        picked = dot(parts[...].reshape(PAIRS * 16, 256), one_hot)
        pairs = pair_of[:, cols]
        values = jnp.zeros((16, CHUNK), F32)
        for pair in range(PAIRS):
            values = jnp.where(pairs == pair, picked[16 * pair : 16 * pair + 16], values)
        values = values[:8] + values[8:]
        given = []
        for s in range(CHUNK_SLOTS):
            product = dot(two_parts(values[:, s * PTS : (s + 1) * PTS]), operator[c * CHUNK_SLOTS + s])
            given.append(
                two_parts(product[:8, :PTS] + (product[:8, PTS:] + product[8:, :PTS]))
            )
        given = jnp.concatenate(given, axis=1)
        pairs = pair_of16[:, cols]
        nothing = jnp.zeros_like(given)
        spread = [jnp.where(pairs == pair, given, nothing) for pair in range(PAIRS)]
        term = dot_t(jnp.concatenate(spread, axis=0), one_hot)
        if c == 0:
            added[g] = term
        else:
            added[g] += term

    def stencil_plane(turn, g, x, diagonal):
        own = [field[turn, g, x * SY + y] for y in range(SY)]
        ring = own + [other_y[turn, g, x * SY + y] for y in range(SY)]
        for y in range(SY):
            value = own[y]
            total = value * (jnp.broadcast_to(pot[pl.ds(x * SY + y, 1)], (GB, SZ)) + diagonal)
            for k in range(1, WIDTH + 1):
                near = ring[(y + k) % (2 * SY)] + ring[(y - k) % (2 * SY)]
                near += pltpu.roll(value, k, axis=1) + pltpu.roll(value, SZ - k, axis=1)
                if x - k >= 0:
                    near += field[turn, g, (x - k) * SY + y]
                if x + k < SX:
                    near += field[turn, g, (x + k) * SY + y]
                total += (KINETIC * LAP_COEFFS[k]) * near
            local[g, x * SY + y] = total

    def apply_local(step, turn, g):
        diagonal = 3.0 * KINETIC * LAP_COEFFS[0] - chosen(step, SHIFT)
        nonlocal_chunk(g, 0)
        nonlocal_chunk(g, 1)
        halo_copies(turn, g)[2].wait_recv()
        nonlocal_chunk(g, 2)
        for x in range(4):
            stencil_plane(turn, g, x, diagonal)
        nonlocal_chunk(g, 3)
        for x in range(4, 8):
            stencil_plane(turn, g, x, diagonal)

    def finish(step, turn, g):
        scale, carry = chosen(step, SCALE), chosen(step, CARRY)
        for y in range(0, SY, 2):
            lower = [[low_x[turn, g, j * SY + y + e] for j in range(WIDTH)] for e in range(2)]
            upper = [[high_x[turn, g, j * SY + y + e] for j in range(WIDTH)] for e in range(2)]
            for x in range(SX):
                pair = x * (SY // 2) + y // 2
                spread = added[g, pl.ds(16 * pair, 16)]
                spread = spread[:8] + spread[8:]
                new = []
                for e in range(2):
                    row = x * SY + y + e
                    total = local[g, row] + spread[:, e * SZ : (e + 1) * SZ]
                    for j in range(WIDTH):
                        if j >= x:
                            total += (KINETIC * LAP_COEFFS[x + WIDTH - j]) * lower[e][j]
                        if j <= x - 2:
                            total += (KINETIC * LAP_COEFFS[SX + j - x]) * upper[e][j]
                    value = scale * total + carry * field[1 - turn, g, row]
                    field[1 - turn, g, row] = value
                    new.append(value)
                split_pair(pair, new[0], new[1])

    for g in range(groups):
        for pair in range(PAIRS):
            split_pair(pair, field[0, g, 2 * pair], field[0, g, 2 * pair + 1])
        apply_local(0, 0, g)

    @pl.loop(0, STEPS * groups)
    def _(at):
        step = at // groups
        g = lax.rem(at, groups)
        turn = lax.rem(step, 2)
        copies = halo_copies(turn, g)
        copies[0].wait()
        copies[1].wait()
        copies[2].wait_send()
        finish(step, turn, g)

        @pl.when(step < STEPS - 1)
        def _():
            for copy in halo_copies(1 - turn, g):
                copy.start()
            apply_local(step + 1, 1 - turn, g)

        @pl.when(step == STEPS - 1)
        def _():
            band_copy(g).start()

    bands = groups * GB
    for g in range(groups):
        for b in range(GB):
            for x in range(SX):
                ready[g * GB + b, pl.ds(x * SY, SY)] = field[0, g, pl.ds(x * SY, SY), b, :]
    store = loaded(ready, out, groups)
    store.start()

    @pl.loop(0, ROWS, unroll=8)
    def _(row):
        cols = pl.ds(pl.multiple_of(row * SZ, SZ), SZ)
        wide[:, cols] = two_parts(jnp.concatenate([field[0, g, row] for g in range(groups)], axis=0))

    def folded(product):
        return (product[:bands, :bands] + product[bands:, bands:]) + (
            product[:bands, bands:] + product[bands:, :bands]
        )

    block = wide[...]
    sums[0, :, :bands] = folded(dot_t(block, block))
    for g in range(groups):
        band_copy(g).wait()

    @pl.loop(0, ROWS // 2, unroll=8)
    def _(row):
        cols = pl.ds(pl.multiple_of(row * SZ, SZ), SZ)
        wide_other[:, cols] = two_parts(
            jnp.concatenate([other_band[g, row] for g in range(groups)], axis=0)
        )

    half = ROWS // 2 * SZ
    kept = wide[:, pl.ds(pl.multiple_of((1 - band) * half, half), half)]
    came = wide_other[...]
    sums[0, :, bands : 2 * bands] = folded(dot_t(kept, came))
    sums[0, :, 2 * bands : 3 * bands] = folded(dot_t(came, kept))

    used = 0
    for at, phase in enumerate(phases):
        copies = []
        for device in phase:
            copies.append(
                pltpu.make_async_remote_copy(
                    src_ref=sums.at[at],
                    dst_ref=sums_in.at[used],
                    send_sem=send_sums.at[used],
                    recv_sem=recv_sums.at[used],
                    device_id=device,
                    device_id_type=MESH,
                )
            )
            copies[-1].start()
            used += 1
        for copy in copies:
            copy.wait()
        total = sums[at]
        if at + 1 < len(phases):
            for n in range(len(phase)):
                total += sums_in[used - len(phase) + n]
            sums[at + 1] = total

    other = jnp.zeros_like(total)
    for n in range(len(phases[-1])):
        came = sums_in[used - len(phases[-1]) + n]
        place = lax.rem(ring + 2 * depth - (n + 1), 2 * depth)
        same = jnp.full(came.shape, place // depth, jnp.int32) == band
        total += jnp.where(same, came, 0.0)
        other += jnp.where(same, 0.0, came)
    own = total[:, :bands]
    mixed = total[:, bands : 2 * bands] + other[:, 2 * bands : 3 * bands]
    first = jnp.full(own.shape, band, jnp.int32) == 0
    weight = 1.0 / (tiles * ROWS * SZ)
    gram[:, :bands] = jnp.where(first, own, mixed) * weight
    gram[:, bands:] = jnp.where(first, mixed, own) * weight
    store.wait()


def per_device(tiles, psi, potential, projector, coupling, slot_live, point_count, point_index):
    bands = psi.shape[0]
    groups = bands // GB
    hbm = pl.BlockSpec(memory_space=pltpu.HBM)
    vmem = pl.BlockSpec(memory_space=pltpu.VMEM)
    filtered, gram = pl.pallas_call(
        functools.partial(kernel, tiles),
        out_shape=(
            jax.ShapeDtypeStruct((bands, ROWS, SZ), F32),
            jax.ShapeDtypeStruct((bands, 2 * bands), F32),
        ),
        in_specs=[hbm] * 7,
        out_specs=(hbm, vmem),
        scratch_shapes=[
            pltpu.VMEM((bands, ROWS, SZ), F32),
            pltpu.VMEM((bands, ROWS, SZ), F32),
            pltpu.VMEM((ROWS, SZ), F32),
            pltpu.VMEM((SLOTS, NPROJ, PTS), F32),
            pltpu.VMEM((NPROJ, SLOTS), F32),
            pltpu.SMEM((1,), jnp.int32),
            pltpu.SMEM((SLOTS,), jnp.int32),
            pltpu.VMEM((SLOTS, PTS), jnp.int32),
            pltpu.VMEM((2, groups, ROWS, GB, SZ), F32),
            pltpu.VMEM((2, groups, WIDTH * SY, GB, SZ), F32),
            pltpu.VMEM((2, groups, WIDTH * SY, GB, SZ), F32),
            pltpu.VMEM((2, groups, ROWS, GB, SZ), F32),
            pltpu.VMEM((groups, ROWS // 2, GB, SZ), F32),
            pltpu.VMEM((256, POINTS), BF16),
            pltpu.VMEM((16, POINTS), jnp.int32),
            pltpu.VMEM((16, POINTS), BF16),
            pltpu.VMEM((SLOTS, PTS, 2 * PTS), BF16),
            pltpu.VMEM((PAIRS, 16, 256), BF16),
            pltpu.VMEM((groups, PAIRS * 16, 256), F32),
            pltpu.VMEM((groups, ROWS, GB, SZ), F32),
            pltpu.VMEM((2 * bands, ROWS * SZ), BF16),
            pltpu.VMEM((2 * bands, ROWS * SZ // 2), BF16),
            pltpu.SemaphoreType.DMA((2, groups, 3)),
            pltpu.SemaphoreType.DMA((2, groups, 3)),
            pltpu.SemaphoreType.DMA((groups,)),
            pltpu.SemaphoreType.DMA((groups,)),
            pltpu.VMEM((4, bands, 128), F32),
            pltpu.VMEM((14, bands, 128), F32),
            pltpu.SemaphoreType.DMA((14,)),
            pltpu.SemaphoreType.DMA((14,)),
            pltpu.SemaphoreType.DMA((groups + 6,)),
        ],
        compiler_params=pltpu.CompilerParams(
            collective_id=0, has_side_effects=True, vmem_limit_bytes=62 << 20
        ),
        name="filter",
    )(
        psi.reshape(bands, ROWS, SZ),
        potential.reshape(ROWS, SZ),
        projector[0],
        jnp.swapaxes(coupling, 1, 2)[0],
        slot_live,
        point_count[0],
        point_index[0],
    )
    return filtered.reshape(psi.shape), gram


def solution(mesh):
    placed = (
        P("band", "space", None, None, None),
        P("space", None, None, None),
        P("space", None, None, None),
        P("space", None, None),
        P("space"),
        P("space", None),
        P("space", None, None),
    )
    return jax.shard_map(
        functools.partial(per_device, mesh.shape["space"]),
        mesh=mesh,
        in_specs=placed,
        out_specs=(P("band", "space", None, None, None), P("band", None)),
        check_vma=False,
    )
```

```python
import functools

import jax
import jax.numpy as jnp
from jax import lax
from jax.experimental import pallas as pl
from jax.experimental.pallas import tpu as pltpu
from jax.sharding import PartitionSpec as P

LAP_COEFFS = (
    -5369.0 / 1800.0,
    12.0 / 7.0,
    -15.0 / 56.0,
    10.0 / 189.0,
    -1.0 / 112.0,
    2.0 / 1925.0,
    -1.0 / 16632.0,
)
KINETIC = -2.0
FILTERS = ((10.0, 60.0, -2.0), (6.0, 60.0, -2.0))
WIDTH = 6
MESH = pl.DeviceIdType.MESH
F32, BF16 = jnp.float32, jnp.bfloat16

SX, SY, SZ = 8, 8, 128
ROWS = SX * SY
GB = 8
LOT = 4
LOTS = ROWS // LOT
PLACES = LOT * SZ
SLOTS, NPROJ, PTS = 32, 16, 128
POINTS = SLOTS * PTS
CHUNK = 512
PIECES = POINTS // CHUNK
STEPS = 4


def step_constants():
    scale, carry, shift = [], [], []
    for low, high, bottom in FILTERS:
        half = (high - low) / 2.0
        centre = (high + low) / 2.0
        sigma = half / (bottom - centre)
        tau = 2.0 / sigma
        following = 1.0 / (tau - sigma)
        scale += [sigma / half, 2.0 * following / half]
        carry += [0.0, -sigma * following]
        shift += [centre, centre]
    return scale, carry, shift


SCALE, CARRY, SHIFT = step_constants()


def chosen(step, values):
    out = jnp.float32(values[-1])
    for at in range(len(values) - 2, -1, -1):
        out = jnp.where(step == at, jnp.float32(values[at]), out)
    return out


def two_parts(value):
    high = value.astype(BF16).astype(F32)
    return jnp.concatenate([high, value - high], axis=0).astype(BF16)


def dot(a, b):
    return jnp.dot(a, b, preferred_element_type=F32)


def dot_t(a, b):
    return lax.dot_general(a, b, (((1,), (1,)), ((), ())), preferred_element_type=F32)


def kernel(
    tiles,
    psi_in,
    pot_in,
    projector_in,
    coupling_in,
    slot_live_in,
    point_count_in,
    point_index_in,
    out,
    gram,
    ready,
    psi,
    pot,
    projector,
    coupling,
    slot_live,
    point_count,
    point_index,
    field,
    low_x,
    high_x,
    other_y,
    other_band,
    hot,
    lot_of,
    lot_of16,
    operator,
    parts,
    added,
    given,
    local,
    wide,
    wide_other,
    send,
    recv,
    send_band,
    recv_band,
    sums,
    sums_in,
    send_sums,
    recv_sums,
    load,
):
    groups = field.shape[1]
    band = lax.axis_index("band")
    tile = lax.axis_index("space")
    up = (band, lax.rem(tile + 2, tiles))
    down = (band, lax.rem(tile + tiles - 2, tiles))
    beside = (band, tile + 1 - 2 * lax.rem(tile, 2))
    across = (1 - band, tile)

    def turned_by(span, low, away):
        return (band, tile - lax.rem(tile, span) + lax.rem(lax.rem(tile, span) + away * low, span))

    depth = tiles // 32
    ring = band * depth + tile // 32

    def along(away):
        place = lax.rem(ring + away, 2 * depth)
        return (place // depth, lax.rem(place, depth) * 32 + lax.rem(tile, 32))

    phases = (
        [beside],
        [turned_by(32, 2, away) for away in range(1, 16)],
        [along(away) for away in range(1, 2 * depth)],
    )

    barrier = pltpu.get_barrier_semaphore()
    greeted = [up, down] + [device for phase in phases for device in phase]
    for device in greeted:
        pl.semaphore_signal(barrier, inc=1, device_id=device, device_id_type=MESH)

    def loaded(src, dst, at):
        return pltpu.make_async_copy(src, dst, load.at[at])

    loads = [
        loaded(psi_in.at[pl.ds(g * GB, GB)], psi.at[pl.ds(g * GB, GB)], g) for g in range(groups)
    ] + [
        loaded(src, dst, groups + at)
        for at, (src, dst) in enumerate(
            (
                (point_index_in, point_index),
                (projector_in, projector),
                (coupling_in, coupling),
                (slot_live_in, slot_live),
                (point_count_in, point_count),
                (pot_in, pot),
            )
        )
    ]
    for copy in loads:
        copy.start()

    def halo_copies(turn, g):
        def copy(src, dst, which, device):
            return pltpu.make_async_remote_copy(
                src_ref=src,
                dst_ref=dst,
                send_sem=send.at[turn, g, which],
                recv_sem=recv.at[turn, g, which],
                device_id=device,
                device_id_type=MESH,
            )

        block = field.at[turn, g]
        copies = []
        for half in range(2):
            rows = pl.ds(half * LOT, LOT)
            copies += [
                copy(
                    block.at[pl.ds(SX - WIDTH, WIDTH), rows],
                    low_x.at[turn, g, :, rows],
                    2 * half,
                    up,
                ),
                copy(block.at[pl.ds(0, WIDTH), rows], high_x.at[turn, g, :, rows], 2 * half + 1, down),
            ]
        return copies + [copy(block, other_y.at[turn, g], 4, beside)]

    def band_copy(g):
        return pltpu.make_async_remote_copy(
            src_ref=field.at[0, g, pl.ds(band * (SX // 2), SX // 2)],
            dst_ref=other_band.at[g],
            send_sem=send_band.at[g],
            recv_sem=recv_band.at[g],
            device_id=across,
            device_id_type=MESH,
        )

    def split_lot(g, lot, rows):
        parts[g, lot] = two_parts(jnp.concatenate(rows, axis=1))

    for g in range(groups):
        loads[g].wait()
        for b in range(GB):
            for x in range(SX):
                field[0, g, x, :, b, :] = psi[g * GB + b, pl.ds(x * SY, SY)]
        if g == 0:
            pl.semaphore_wait(barrier, len(greeted))
        for copy in halo_copies(0, g):
            copy.start()

    field[1] = jnp.zeros(field.shape[1:], F32)
    for copy in loads[groups:]:
        copy.wait()

    @pl.loop(0, SLOTS, unroll=8)
    def _(s):
        cols = pl.ds(pl.multiple_of(s * PTS, PTS), PTS)
        index = point_index[pl.ds(s, 1), :]
        place = jnp.broadcast_to(index & (PLACES - 1), (PLACES, PTS))
        spots = lax.broadcasted_iota(jnp.int32, (PLACES, PTS), 0)
        hot[:, cols] = jnp.where(place == spots, 1.0, 0.0).astype(BF16)
        lot = jnp.broadcast_to(index // PLACES, (16, PTS))
        lot_of[:, cols] = lot
        lot_of16[:, cols] = lot.astype(F32).astype(BF16)
        points = lax.broadcasted_iota(jnp.int32, (NPROJ, PTS), 1)
        slots = jnp.full((NPROJ, PTS), s, jnp.int32)
        keep = (points < point_count[s]) & (slots < slot_live[0])
        weights = jnp.where(keep, projector[s], 0.0)
        mine = lax.broadcasted_iota(jnp.int32, (NPROJ, SLOTS), 1) == s
        couple = jnp.sum(jnp.where(mine, coupling[...], 0.0), axis=1, keepdims=True)
        coupled = weights * couple
        weights_high = weights.astype(BF16).astype(F32)
        coupled_high = coupled.astype(BF16).astype(F32)
        left = jnp.concatenate([weights_high, weights_high, weights - weights_high], axis=0)
        right = jnp.concatenate([coupled_high, coupled - coupled_high, coupled_high], axis=0)
        square = dot(left.T.astype(BF16), right.astype(BF16))
        square_high = square.astype(BF16).astype(F32)
        operator[s] = jnp.concatenate([square_high, square - square_high], axis=1).astype(BF16)

    def gathered(g, piece):
        cols = pl.ds(piece * CHUNK, CHUNK)
        picked = dot(parts[g].reshape(LOTS * 16, PLACES), hot[:, cols])
        lots = lot_of[:, cols]
        values = jnp.zeros((16, CHUNK), F32)
        for lot in range(LOTS):
            values = jnp.where(lots == lot, picked[16 * lot : 16 * lot + 16], values)
        return values[:8] + values[8:]

    def operated(values, piece):
        given = []
        nothing = jnp.zeros((16, PTS), BF16)
        for s in range(0, CHUNK // PTS, 2):
            first = two_parts(values[:, s * PTS : (s + 1) * PTS])
            second = two_parts(values[:, (s + 1) * PTS : (s + 2) * PTS])
            both = jnp.concatenate(
                [
                    jnp.concatenate([first, nothing], axis=1),
                    jnp.concatenate([nothing, second], axis=1),
                ],
                axis=0,
            )
            at = piece * (CHUNK // PTS) + s
            products = dot(both, operator[at : at + 2].reshape(2 * PTS, 2 * PTS))
            for product in (products[:16], products[16:]):
                given.append(
                    two_parts(product[:8, :PTS] + (product[:8, PTS:] + product[8:, :PTS]))
                )
        return jnp.concatenate(given, axis=1)

    def gather_and_operate(g):
        values = [gathered(g, piece) for piece in range(PIECES)]
        for piece in range(PIECES):
            given[:, piece * CHUNK : (piece + 1) * CHUNK] = operated(values[piece], piece)

    def scatter():
        amounts = given[...]
        lots = lot_of16[...]
        nothing = jnp.zeros_like(amounts)
        spread = [jnp.where(lots == lot, amounts, nothing) for lot in range(LOTS)]
        added[...] = dot_t(jnp.concatenate(spread, axis=0), hot[...])

    def stencil_plane(turn, g, x, diagonal):
        own = [field[turn, g, x, y] for y in range(SY)]
        ring = own + [other_y[turn, g, x, y] for y in range(SY)]
        for y in range(SY):
            value = own[y]
            total = value * (jnp.broadcast_to(pot[pl.ds(x * SY + y, 1)], (GB, SZ)) + diagonal)
            for k in range(1, WIDTH + 1):
                near = ring[(y + k) % (2 * SY)] + ring[(y - k) % (2 * SY)]
                near += pltpu.roll(value, k, axis=1) + pltpu.roll(value, SZ - k, axis=1)
                if x - k >= 0:
                    near += field[turn, g, x - k, y]
                if x + k < SX:
                    near += field[turn, g, x + k, y]
                total += (KINETIC * LAP_COEFFS[k]) * near
            local[g, x, y] = total

    def finish(step, turn, g, half):
        for copy in halo_copies(turn, g)[2 * half : 2 * half + 2]:
            copy.wait()
        scale, carry = chosen(step, SCALE), chosen(step, CARRY)
        for x in range(SX):
            lot = x * (SY // LOT) + half
            spread = added[pl.ds(16 * lot, 16)]
            spread = spread[:8] + spread[8:]
            new = []
            for e in range(LOT):
                y = half * LOT + e
                total = local[g, x, y] + spread[:, e * SZ : (e + 1) * SZ]
                for j in range(WIDTH):
                    if j >= x:
                        total += (KINETIC * LAP_COEFFS[x + WIDTH - j]) * low_x[turn, g, j, y]
                    if j <= x - 2:
                        total += (KINETIC * LAP_COEFFS[SX + j - x]) * high_x[turn, g, j, y]
                value = scale * total + carry * field[1 - turn, g, x, y]
                field[1 - turn, g, x, y] = value
                new.append(value)
            split_lot(g, lot, new)

        @pl.when(step < STEPS - 1)
        def _():
            following = halo_copies(1 - turn, g)
            for copy in following[2 * half : 2 * half + 2] + following[4:] * half:
                copy.start()

        if half == 1:

            @pl.when(step == STEPS - 1)
            def _():
                band_copy(g).start()

    for g in range(groups):
        for lot in range(LOTS):
            x, half = lot // (SY // LOT), lot % (SY // LOT)
            split_lot(g, lot, [field[0, g, x, half * LOT + e] for e in range(LOT)])

    rounds = STEPS * groups

    def place_of(at):
        step = at // groups
        return step, step % 2, at % groups

    @pl.loop(0, rounds)
    def _(at):
        step, turn, g = place_of(at)
        diagonal = 3.0 * KINETIC * LAP_COEFFS[0] - chosen(step, SHIFT)
        halo_copies(turn, g)[4].wait()
        gather_and_operate(g)
        for x in range(SX // 2):
            stencil_plane(turn, g, x, diagonal)

        @pl.when(at > 0)
        def _():
            finish(*place_of(lax.rem(at + rounds - 1, rounds)), 1)

        scatter()
        for x in range(SX // 2, SX):
            stencil_plane(turn, g, x, diagonal)
        finish(step, turn, g, 0)

    finish(*place_of(rounds - 1), 1)

    bands = groups * GB
    for g in range(groups):
        for b in range(GB):
            for x in range(SX):
                ready[g * GB + b, pl.ds(x * SY, SY)] = field[0, g, x, :, b, :]
    store = loaded(ready, out, groups)
    store.start()

    @pl.loop(0, ROWS, unroll=8)
    def _(row):
        cols = pl.ds(pl.multiple_of(row * SZ, SZ), SZ)
        wide[:, cols] = two_parts(jnp.concatenate([field[0, g, row // SY, row % SY] for g in range(groups)], axis=0))

    def folded(product):
        rows, cols = product.shape[0] // 2, product.shape[1] // 2
        return (product[:rows, :cols] + product[rows:, cols:]) + (
            product[:rows, cols:] + product[rows:, :cols]
        )

    def keep_term(term, row, col):
        for at in range(0, term.shape[0], GB):
            lane = (row + at) // GB * 64 + col
            sums[0, :, lane : lane + term.shape[1]] = term[at : at + GB]

    def kept_term(sum_, col):
        return jnp.concatenate([sum_[:, col : col + bands], sum_[:, 64 + col : 64 + col + bands]], axis=0)

    sums[0] = jnp.zeros(sums.shape[1:], F32)
    block = wide[...]
    keep_term(folded(dot_t(block, block)), 0, 0)

    half = ROWS // 2 * SZ
    kept = wide[:, pl.ds(pl.multiple_of((1 - band) * half, half), half)]
    for g in range(groups):
        band_copy(g).wait()
        for row in range(ROWS // 2):
            wide_other[g, :, row * SZ : (row + 1) * SZ] = two_parts(
                other_band[g, row // SY, row % SY]
            )
        came = wide_other[g]
        keep_term(folded(dot_t(kept, came)), 0, bands + g * GB)
        keep_term(folded(dot_t(came, kept)), g * GB, 2 * bands)

    used = 0
    for at, phase in enumerate(phases):
        copies = []
        for device in phase:
            copies.append(
                pltpu.make_async_remote_copy(
                    src_ref=sums.at[at],
                    dst_ref=sums_in.at[used],
                    send_sem=send_sums.at[used],
                    recv_sem=recv_sums.at[used],
                    device_id=device,
                    device_id_type=MESH,
                )
            )
            copies[-1].start()
            used += 1
        for copy in copies:
            copy.wait()
        total = sums[at]
        if at + 1 < len(phases):
            for n in range(len(phase)):
                total += sums_in[used - len(phase) + n]
            sums[at + 1] = total

    other = jnp.zeros_like(total)
    for n in range(len(phases[-1])):
        came = sums_in[used - len(phases[-1]) + n]
        place = lax.rem(ring + 2 * depth - (n + 1), 2 * depth)
        same = jnp.full(came.shape, place // depth, jnp.int32) == band
        total += jnp.where(same, came, 0.0)
        other += jnp.where(same, 0.0, came)
    own = kept_term(total, 0)
    mixed = kept_term(total, bands) + kept_term(other, 2 * bands)
    first = jnp.full(own.shape, band, jnp.int32) == 0
    weight = 1.0 / (tiles * ROWS * SZ)
    gram[:, :bands] = jnp.where(first, own, mixed) * weight
    gram[:, bands:] = jnp.where(first, mixed, own) * weight
    store.wait()


def per_device(tiles, psi, potential, projector, coupling, slot_live, point_count, point_index):
    bands = psi.shape[0]
    groups = bands // GB
    hbm = pl.BlockSpec(memory_space=pltpu.HBM)
    vmem = pl.BlockSpec(memory_space=pltpu.VMEM)
    filtered, gram = pl.pallas_call(
        functools.partial(kernel, tiles),
        out_shape=(
            jax.ShapeDtypeStruct((bands, ROWS, SZ), F32),
            jax.ShapeDtypeStruct((bands, 2 * bands), F32),
        ),
        in_specs=[hbm] * 7,
        out_specs=(hbm, vmem),
        scratch_shapes=[
            pltpu.VMEM((bands, ROWS, SZ), F32),
            pltpu.VMEM((bands, ROWS, SZ), F32),
            pltpu.VMEM((ROWS, SZ), F32),
            pltpu.VMEM((SLOTS, NPROJ, PTS), F32),
            pltpu.VMEM((NPROJ, SLOTS), F32),
            pltpu.SMEM((1,), jnp.int32),
            pltpu.SMEM((SLOTS,), jnp.int32),
            pltpu.VMEM((SLOTS, PTS), jnp.int32),
            pltpu.VMEM((2, groups, SX, SY, GB, SZ), F32),
            pltpu.VMEM((2, groups, WIDTH, SY, GB, SZ), F32),
            pltpu.VMEM((2, groups, WIDTH, SY, GB, SZ), F32),
            pltpu.VMEM((2, groups, SX, SY, GB, SZ), F32),
            pltpu.VMEM((groups, SX // 2, SY, GB, SZ), F32),
            pltpu.VMEM((PLACES, POINTS), BF16),
            pltpu.VMEM((16, POINTS), jnp.int32),
            pltpu.VMEM((16, POINTS), BF16),
            pltpu.VMEM((SLOTS, PTS, 2 * PTS), BF16),
            pltpu.VMEM((groups, LOTS, 16, PLACES), BF16),
            pltpu.VMEM((LOTS * 16, PLACES), F32),
            pltpu.VMEM((16, POINTS), BF16),
            pltpu.VMEM((groups, SX, SY, GB, SZ), F32),
            pltpu.VMEM((2 * bands, ROWS * SZ), BF16),
            pltpu.VMEM((groups, 2 * GB, ROWS * SZ // 2), BF16),
            pltpu.SemaphoreType.DMA((2, groups, 5)),
            pltpu.SemaphoreType.DMA((2, groups, 5)),
            pltpu.SemaphoreType.DMA((groups,)),
            pltpu.SemaphoreType.DMA((groups,)),
            pltpu.VMEM((3, GB, 128), F32),
            pltpu.VMEM((23, GB, 128), F32),
            pltpu.SemaphoreType.DMA((23,)),
            pltpu.SemaphoreType.DMA((23,)),
            pltpu.SemaphoreType.DMA((groups + 6,)),
        ],
        compiler_params=pltpu.CompilerParams(
            collective_id=0, has_side_effects=True, vmem_limit_bytes=62 << 20
        ),
        name="filter",
    )(
        psi.reshape(bands, ROWS, SZ),
        potential.reshape(ROWS, SZ),
        projector[0],
        jnp.swapaxes(coupling, 1, 2)[0],
        slot_live,
        point_count[0],
        point_index[0],
    )
    return filtered.reshape(psi.shape), gram


def solution(mesh):
    placed = (
        P("band", "space", None, None, None),
        P("space", None, None, None),
        P("space", None, None, None),
        P("space", None, None),
        P("space"),
        P("space", None),
        P("space", None, None),
    )
    return jax.shard_map(
        functools.partial(per_device, mesh.shape["space"]),
        mesh=mesh,
        in_specs=placed,
        out_specs=(P("band", "space", None, None, None), P("band", None)),
        check_vma=False,
    )
```

```python
import functools

import jax
import jax.numpy as jnp
from jax import lax
from jax.experimental import pallas as pl
from jax.experimental.pallas import tpu as pltpu
from jax.sharding import PartitionSpec as P

LAP_COEFFS = (
    -5369.0 / 1800.0,
    12.0 / 7.0,
    -15.0 / 56.0,
    10.0 / 189.0,
    -1.0 / 112.0,
    2.0 / 1925.0,
    -1.0 / 16632.0,
)
KINETIC = -2.0
FILTERS = ((10.0, 60.0, -2.0), (6.0, 60.0, -2.0))
WIDTH = 6
MESH = pl.DeviceIdType.MESH
F32, BF16 = jnp.float32, jnp.bfloat16

SX, SY, SZ = 8, 8, 128
ROWS = SX * SY
GB = 8
LOT = 4
LOTS = ROWS // LOT
PLACES = LOT * SZ
SLOTS, NPROJ, PTS = 32, 16, 128
POINTS = SLOTS * PTS
CHUNK = 512
PIECES = POINTS // CHUNK
LANE_PIECES = (3, 5, 7)
STEPS = 4


def step_constants():
    scale, carry, shift = [], [], []
    for low, high, bottom in FILTERS:
        half = (high - low) / 2.0
        centre = (high + low) / 2.0
        sigma = half / (bottom - centre)
        tau = 2.0 / sigma
        following = 1.0 / (tau - sigma)
        scale += [sigma / half, 2.0 * following / half]
        carry += [0.0, -sigma * following]
        shift += [centre, centre]
    return scale, carry, shift


SCALE, CARRY, SHIFT = step_constants()


def chosen(step, values):
    out = jnp.float32(values[-1])
    for at in range(len(values) - 2, -1, -1):
        out = jnp.where(step == at, jnp.float32(values[at]), out)
    return out


def two_parts(value):
    high = value.astype(BF16).astype(F32)
    return jnp.concatenate([high, value - high], axis=0).astype(BF16)


def dot(a, b):
    return jnp.dot(a, b, preferred_element_type=F32)


def dot_t(a, b):
    return lax.dot_general(a, b, (((1,), (1,)), ((), ())), preferred_element_type=F32)


def kernel(
    tiles,
    psi_in,
    pot_in,
    projector_in,
    coupling_in,
    slot_live,
    point_count_in,
    point_index_in,
    out,
    gram,
    psi,
    pot,
    projector,
    coupling,
    point_count,
    point_index,
    field,
    low_x,
    high_x,
    other_y,
    other_band,
    hot,
    lot_of,
    lot_of16,
    row_of,
    lane_of,
    operator,
    parts,
    added,
    given,
    local,
    wide,
    wide_other,
    send,
    recv,
    send_band,
    recv_band,
    sums,
    sums_in,
    send_sums,
    recv_sums,
    load,
):
    groups = field.shape[1]
    band = lax.axis_index("band")
    tile = lax.axis_index("space")
    up = (band, lax.rem(tile + 2, tiles))
    down = (band, lax.rem(tile + tiles - 2, tiles))
    beside = (band, tile + 1 - 2 * lax.rem(tile, 2))
    across = (1 - band, tile)

    def turned_by(span, low, away):
        return (band, tile - lax.rem(tile, span) + lax.rem(lax.rem(tile, span) + away * low, span))

    depth = tiles // 32
    ring = band * depth + tile // 32

    def along(away):
        place = lax.rem(ring + away, 2 * depth)
        return (place // depth, lax.rem(place, depth) * 32 + lax.rem(tile, 32))

    phases = (
        [beside],
        [turned_by(32, 2, away) for away in range(1, 16)],
        [along(away) for away in range(1, 2 * depth)],
    )

    barrier = pltpu.get_barrier_semaphore()
    greeted = [up, down] + [device for phase in phases for device in phase]
    for device in greeted:
        pl.semaphore_signal(barrier, inc=1, device_id=device, device_id_type=MESH)

    def loaded(src, dst, at):
        return pltpu.make_async_copy(src, dst, load.at[at])

    loads = [
        loaded(psi_in.at[pl.ds(g * GB, GB)], psi.at[pl.ds(g * GB, GB)], g) for g in range(groups)
    ] + [
        loaded(src, dst, groups + at)
        for at, (src, dst) in enumerate(
            (
                (point_index_in, point_index),
                (projector_in, projector),
                (coupling_in, coupling),
                (point_count_in, point_count),
                (pot_in, pot),
            )
        )
    ]
    for copy in loads:
        copy.start()

    def halo_copies(turn, g):
        def copy(src, dst, which, device):
            return pltpu.make_async_remote_copy(
                src_ref=src,
                dst_ref=dst,
                send_sem=send.at[turn, g, which],
                recv_sem=recv.at[turn, g, which],
                device_id=device,
                device_id_type=MESH,
            )

        block = field.at[turn, g]
        copies = []
        for half in range(2):
            rows = pl.ds(half * LOT, LOT)
            copies += [
                copy(
                    block.at[pl.ds(SX - WIDTH, WIDTH), rows],
                    low_x.at[turn, g, :, rows],
                    2 * half,
                    up,
                ),
                copy(block.at[pl.ds(0, WIDTH), rows], high_x.at[turn, g, :, rows], 2 * half + 1, down),
            ]
        return copies + [copy(block, other_y.at[turn, g], 4, beside)]

    def band_copy(g, half):
        rows = pl.ds(half * LOT, LOT)
        return pltpu.make_async_remote_copy(
            src_ref=field.at[0, g, pl.ds(band * (SX // 2), SX // 2), rows],
            dst_ref=other_band.at[g, :, rows],
            send_sem=send_band.at[g, half],
            recv_sem=recv_band.at[g, half],
            device_id=across,
            device_id_type=MESH,
        )

    def split_lot(g, lot, rows):
        parts[g, lot] = two_parts(jnp.concatenate(rows, axis=1))

    for g in range(groups):
        loads[g].wait()
        for b in range(GB):
            for x in range(SX):
                field[0, g, x, :, b, :] = psi[g * GB + b, pl.ds(x * SY, SY)]
        if g == 0:
            pl.semaphore_wait(barrier, len(greeted))
        for copy in halo_copies(0, g):
            copy.start()

    field[1] = jnp.zeros(field.shape[1:], F32)
    for copy in loads[groups:]:
        copy.wait()

    @pl.loop(0, SLOTS, unroll=8)
    def _(s):
        cols = pl.ds(pl.multiple_of(s * PTS, PTS), PTS)
        index = point_index[pl.ds(s, 1), :]
        place = jnp.broadcast_to(index & (PLACES - 1), (PLACES, PTS))
        spots = lax.broadcasted_iota(jnp.int32, (PLACES, PTS), 0)
        hot[:, cols] = jnp.where(place == spots, 1.0, 0.0).astype(BF16)
        row_of[:, cols] = jnp.broadcast_to(index // SZ, (GB, PTS))
        lane_of[:, cols] = jnp.broadcast_to(index & (SZ - 1), (GB, PTS))
        lot = jnp.broadcast_to(index // PLACES, (16, PTS))
        lot_of[:, cols] = lot
        lot_of16[:, cols] = lot.astype(F32).astype(BF16)
        points = lax.broadcasted_iota(jnp.int32, (NPROJ, PTS), 1)
        slots = jnp.full((NPROJ, PTS), s, jnp.int32)
        keep = (points < point_count[s]) & (slots < slot_live[0])
        weights = jnp.where(keep, projector[s], 0.0)
        mine = lax.broadcasted_iota(jnp.int32, (NPROJ, SLOTS), 1) == s
        couple = jnp.sum(jnp.where(mine, coupling[...], 0.0), axis=1, keepdims=True)
        coupled = weights * couple
        weights_high = weights.astype(BF16).astype(F32)
        coupled_high = coupled.astype(BF16).astype(F32)
        left = jnp.concatenate([weights_high, weights_high, weights - weights_high], axis=0)
        right = jnp.concatenate([coupled_high, coupled - coupled_high, coupled_high], axis=0)
        square = dot(left.T.astype(BF16), right.astype(BF16))
        square_high = square.astype(BF16).astype(F32)
        operator[s] = jnp.concatenate([square_high, square - square_high], axis=1).astype(BF16)

    def gathered(g, piece):
        cols = pl.ds(piece * CHUNK, CHUNK)
        picked = dot(parts[g].reshape(LOTS * 16, PLACES), hot[:, cols])
        lots = lot_of[:, cols]
        values = jnp.zeros((16, CHUNK), F32)
        for lot in range(LOTS):
            values = jnp.where(lots == lot, picked[16 * lot : 16 * lot + 16], values)
        return values[:8] + values[8:]

    def gathered_by_lanes(turn, g, piece):
        values = []
        for s in range(CHUNK // PTS):
            cols = pl.ds(piece * CHUNK + s * PTS, PTS)
            lanes, rows = lane_of[:, cols], row_of[:, cols]
            found = jnp.zeros((GB, PTS), F32)
            for row in range(ROWS):
                picked = jnp.take_along_axis(
                    field[turn, g, row // SY, row % SY], lanes, axis=1, mode="promise_in_bounds"
                )
                found = jnp.where(rows == row, picked, found)
            values.append(found)
        return jnp.concatenate(values, axis=1)

    def operated(values, piece):
        given = []
        nothing = jnp.zeros((16, PTS), BF16)
        for s in range(0, CHUNK // PTS, 2):
            first = two_parts(values[:, s * PTS : (s + 1) * PTS])
            second = two_parts(values[:, (s + 1) * PTS : (s + 2) * PTS])
            both = jnp.concatenate(
                [
                    jnp.concatenate([first, nothing], axis=1),
                    jnp.concatenate([nothing, second], axis=1),
                ],
                axis=0,
            )
            at = piece * (CHUNK // PTS) + s
            products = dot(both, operator[at : at + 2].reshape(2 * PTS, 2 * PTS))
            for product in (products[:16], products[16:]):
                given.append(
                    two_parts(product[:8, :PTS] + (product[:8, PTS:] + product[8:, :PTS]))
                )
        return jnp.concatenate(given, axis=1)

    def gather_and_operate(turn, g):
        values = [
            gathered_by_lanes(turn, g, piece) if piece in LANE_PIECES else gathered(g, piece)
            for piece in range(PIECES)
        ]
        for piece in range(PIECES):
            given[:, piece * CHUNK : (piece + 1) * CHUNK] = operated(values[piece], piece)

    def scatter():
        amounts = given[...]
        lots = lot_of16[...]
        nothing = jnp.zeros_like(amounts)
        spread = [jnp.where(lots == lot, amounts, nothing) for lot in range(LOTS)]
        added[...] = dot_t(jnp.concatenate(spread, axis=0), hot[...])

    def stencil_plane(turn, g, x, diagonal):
        own = [field[turn, g, x, y] for y in range(SY)]
        ring = own + [other_y[turn, g, x, y] for y in range(SY)]
        for y in range(SY):
            value = own[y]
            total = value * (jnp.broadcast_to(pot[pl.ds(x * SY + y, 1)], (GB, SZ)) + diagonal)
            for k in range(1, WIDTH + 1):
                near = ring[(y + k) % (2 * SY)] + ring[(y - k) % (2 * SY)]
                near += pltpu.roll(value, k, axis=1) + pltpu.roll(value, SZ - k, axis=1)
                if x - k >= 0:
                    near += field[turn, g, x - k, y]
                if x + k < SX:
                    near += field[turn, g, x + k, y]
                total += (KINETIC * LAP_COEFFS[k]) * near
            local[g, x, y] = total

    def finish(step, turn, g, half):
        for copy in halo_copies(turn, g)[2 * half : 2 * half + 2]:
            copy.wait()
        scale, carry = chosen(step, SCALE), chosen(step, CARRY)
        for x in range(SX):
            lot = x * (SY // LOT) + half
            spread = added[pl.ds(16 * lot, 16)]
            spread = spread[:8] + spread[8:]
            new = []
            for e in range(LOT):
                y = half * LOT + e
                total = local[g, x, y] + spread[:, e * SZ : (e + 1) * SZ]
                for j in range(WIDTH):
                    if j >= x:
                        total += (KINETIC * LAP_COEFFS[x + WIDTH - j]) * low_x[turn, g, j, y]
                    if j <= x - 2:
                        total += (KINETIC * LAP_COEFFS[SX + j - x]) * high_x[turn, g, j, y]
                value = scale * total + carry * field[1 - turn, g, x, y]
                field[1 - turn, g, x, y] = value
                new.append(value)
            split_lot(g, lot, new)

        @pl.when(step < STEPS - 1)
        def _():
            following = halo_copies(1 - turn, g)
            for copy in following[2 * half : 2 * half + 2] + following[4:] * half:
                copy.start()

        @pl.when(step == STEPS - 1)
        def _():
            band_copy(g, half).start()

    for g in range(groups):
        for lot in range(LOTS):
            x, half = lot // (SY // LOT), lot % (SY // LOT)
            split_lot(g, lot, [field[0, g, x, half * LOT + e] for e in range(LOT)])

    rounds = STEPS * groups

    def place_of(at):
        step = at // groups
        return step, step % 2, at % groups

    @pl.loop(0, rounds)
    def _(at):
        step, turn, g = place_of(at)
        diagonal = 3.0 * KINETIC * LAP_COEFFS[0] - chosen(step, SHIFT)
        halo_copies(turn, g)[4].wait()
        gather_and_operate(turn, g)
        for x in range(SX // 2):
            stencil_plane(turn, g, x, diagonal)

        @pl.when(at > 0)
        def _():
            finish(*place_of(lax.rem(at + rounds - 1, rounds)), 1)

        scatter()
        for x in range(SX // 2, SX):
            stencil_plane(turn, g, x, diagonal)
        finish(step, turn, g, 0)

    finish(*place_of(rounds - 1), 1)

    bands = groups * GB
    for g in range(groups):
        for b in range(GB):
            for x in range(SX):
                out[g * GB + b, pl.ds(x * SY, SY)] = field[0, g, x, :, b, :]
    quarter = ROWS // 4

    def quarter_rows():
        return [(x, y) for x in range(SX // 2) for y in range(LOT)]

    for at in range(4):
        for n, (x, y) in enumerate(quarter_rows()):
            x, y = x + at // 2 * (SX // 2), y + at % 2 * LOT
            row = at * quarter + n
            wide[:, row * SZ : (row + 1) * SZ] = two_parts(
                jnp.concatenate([field[0, g, x, y] for g in range(groups)], axis=0)
            )

    def folded(product):
        rows, cols = product.shape[0] // 2, product.shape[1] // 2
        return (product[:rows, :cols] + product[rows:, cols:]) + (
            product[:rows, cols:] + product[rows:, :cols]
        )

    def keep_term(term, row, col):
        for at in range(0, term.shape[0], GB):
            lane = (row + at) // GB * 64 + col
            sums[0, :, lane : lane + term.shape[1]] = term[at : at + GB]

    def kept_term(sum_, col):
        return jnp.concatenate([sum_[:, col : col + bands], sum_[:, 64 + col : 64 + col + bands]], axis=0)

    sums[0] = jnp.zeros(sums.shape[1:], F32)
    block = wide[...]
    keep_term(folded(dot_t(block, block)), 0, 0)

    depth_of = quarter * SZ
    for g in range(groups):
        term = None
        for half in range(2):
            start = (2 * (1 - band) + half) * depth_of
            kept = wide[:, pl.ds(pl.multiple_of(start, depth_of), depth_of)]
            band_copy(g, half).wait()
            for n, (x, y) in enumerate(quarter_rows()):
                wide_other[:, n * SZ : (n + 1) * SZ] = two_parts(
                    other_band[g, x, half * LOT + y]
                )
            part = dot_t(kept, wide_other[...])
            term = part if term is None else term + part
        keep_term(folded(term), 0, bands + g * GB)

    used = 0
    for at, phase in enumerate(phases):
        copies = []
        for device in phase:
            copies.append(
                pltpu.make_async_remote_copy(
                    src_ref=sums.at[at],
                    dst_ref=sums_in.at[used],
                    send_sem=send_sums.at[used],
                    recv_sem=recv_sums.at[used],
                    device_id=device,
                    device_id_type=MESH,
                )
            )
            copies[-1].start()
            used += 1
        for copy in copies:
            copy.wait()
        total = sums[at]
        if at + 1 < len(phases):
            for n in range(len(phase)):
                total += sums_in[used - len(phase) + n]
            sums[at + 1] = total

    other = jnp.zeros_like(total)
    for n in range(len(phases[-1])):
        came = sums_in[used - len(phases[-1]) + n]
        place = lax.rem(ring + 2 * depth - (n + 1), 2 * depth)
        same = jnp.full(came.shape, place // depth, jnp.int32) == band
        total += jnp.where(same, came, 0.0)
        other += jnp.where(same, 0.0, came)
    own = kept_term(total, 0)
    mixed = kept_term(total, bands) + kept_term(other, bands).T
    first = jnp.full(own.shape, band, jnp.int32) == 0
    weight = 1.0 / (tiles * ROWS * SZ)
    gram[:, :bands] = jnp.where(first, own, mixed) * weight
    gram[:, bands:] = jnp.where(first, mixed, own) * weight


def in_hbm(array):
    return pltpu.with_memory_space_constraint(array, pltpu.HBM)


def per_device(tiles, psi, potential, projector, coupling, slot_live, point_count, point_index):
    bands = psi.shape[0]
    groups = bands // GB
    hbm = pl.BlockSpec(memory_space=pltpu.HBM)
    vmem = pl.BlockSpec(memory_space=pltpu.VMEM)
    smem = pl.BlockSpec(memory_space=pltpu.SMEM)
    filtered, gram = pl.pallas_call(
        functools.partial(kernel, tiles),
        out_shape=(
            jax.ShapeDtypeStruct((bands, ROWS, SZ), F32),
            jax.ShapeDtypeStruct((bands, 2 * bands), F32),
        ),
        in_specs=[hbm] * 4 + [smem] + [hbm] * 2,
        out_specs=(vmem, vmem),
        scratch_shapes=[
            pltpu.VMEM((bands, ROWS, SZ), F32),
            pltpu.VMEM((ROWS, SZ), F32),
            pltpu.VMEM((SLOTS, NPROJ, PTS), F32),
            pltpu.VMEM((NPROJ, SLOTS), F32),
            pltpu.SMEM((SLOTS,), jnp.int32),
            pltpu.VMEM((SLOTS, PTS), jnp.int32),
            pltpu.VMEM((2, groups, SX, SY, GB, SZ), F32),
            pltpu.VMEM((2, groups, WIDTH, SY, GB, SZ), F32),
            pltpu.VMEM((2, groups, WIDTH, SY, GB, SZ), F32),
            pltpu.VMEM((2, groups, SX, SY, GB, SZ), F32),
            pltpu.VMEM((groups, SX // 2, SY, GB, SZ), F32),
            pltpu.VMEM((PLACES, POINTS), BF16),
            pltpu.VMEM((16, POINTS), jnp.int32),
            pltpu.VMEM((16, POINTS), BF16),
            pltpu.VMEM((GB, POINTS), jnp.int32),
            pltpu.VMEM((GB, POINTS), jnp.int32),
            pltpu.VMEM((SLOTS, PTS, 2 * PTS), BF16),
            pltpu.VMEM((groups, LOTS, 16, PLACES), BF16),
            pltpu.VMEM((LOTS * 16, PLACES), F32),
            pltpu.VMEM((16, POINTS), BF16),
            pltpu.VMEM((groups, SX, SY, GB, SZ), F32),
            pltpu.VMEM((2 * bands, ROWS * SZ), BF16),
            pltpu.VMEM((2 * GB, ROWS * SZ // 4), BF16),
            pltpu.SemaphoreType.DMA((2, groups, 5)),
            pltpu.SemaphoreType.DMA((2, groups, 5)),
            pltpu.SemaphoreType.DMA((groups, 2)),
            pltpu.SemaphoreType.DMA((groups, 2)),
            pltpu.VMEM((3, GB, 128), F32),
            pltpu.VMEM((23, GB, 128), F32),
            pltpu.SemaphoreType.DMA((23,)),
            pltpu.SemaphoreType.DMA((23,)),
            pltpu.SemaphoreType.DMA((groups + 6,)),
        ],
        compiler_params=pltpu.CompilerParams(
            collective_id=0, has_side_effects=True, vmem_limit_bytes=40 << 20
        ),
        name="filter",
    )(
        in_hbm(psi.reshape(bands, ROWS, SZ)),
        in_hbm(potential.reshape(ROWS, SZ)),
        in_hbm(projector[0]),
        in_hbm(jnp.swapaxes(coupling, 1, 2)[0]),
        slot_live,
        in_hbm(point_count[0]),
        in_hbm(point_index[0]),
    )
    return filtered.reshape(psi.shape), gram


def solution(mesh):
    placed = (
        P("band", "space", None, None, None),
        P("space", None, None, None),
        P("space", None, None, None),
        P("space", None, None),
        P("space"),
        P("space", None),
        P("space", None, None),
    )
    return jax.shard_map(
        functools.partial(per_device, mesh.shape["space"]),
        mesh=mesh,
        in_specs=placed,
        out_specs=(P("band", "space", None, None, None), P("band", None)),
        check_vma=False,
    )
```

```python
import functools

import jax
import jax.numpy as jnp
from jax import lax
from jax.experimental import pallas as pl
from jax.experimental.pallas import tpu as pltpu
from jax.sharding import PartitionSpec as P

LAP_COEFFS = (
    -5369.0 / 1800.0,
    12.0 / 7.0,
    -15.0 / 56.0,
    10.0 / 189.0,
    -1.0 / 112.0,
    2.0 / 1925.0,
    -1.0 / 16632.0,
)
KINETIC = -2.0
FILTERS = ((10.0, 60.0, -2.0), (6.0, 60.0, -2.0))
WIDTH = 6
MESH = pl.DeviceIdType.MESH
F32, BF16 = jnp.float32, jnp.bfloat16

SX, SY, SZ = 8, 8, 128
ROWS = SX * SY
GB = 8
LOT = 4
LOTS = ROWS // LOT
PLACES = LOT * SZ
SLOTS, NPROJ, PTS = 32, 16, 128
POINTS = SLOTS * PTS
CHUNK = 512
PIECES = POINTS // CHUNK
LANE_PIECES = (3, 5, 7)
STEPS = 4


def step_constants():
    scale, carry, shift = [], [], []
    for low, high, bottom in FILTERS:
        half = (high - low) / 2.0
        centre = (high + low) / 2.0
        sigma = half / (bottom - centre)
        tau = 2.0 / sigma
        following = 1.0 / (tau - sigma)
        scale += [sigma / half, 2.0 * following / half]
        carry += [0.0, -sigma * following]
        shift += [centre, centre]
    return scale, carry, shift


SCALE, CARRY, SHIFT = step_constants()


def chosen(step, values):
    out = jnp.float32(values[-1])
    for at in range(len(values) - 2, -1, -1):
        out = jnp.where(step == at, jnp.float32(values[at]), out)
    return out


def two_parts(value):
    high = value.astype(BF16).astype(F32)
    return jnp.concatenate([high, value - high], axis=0).astype(BF16)


def dot(a, b):
    return jnp.dot(a, b, preferred_element_type=F32)


def dot_t(a, b):
    return lax.dot_general(a, b, (((1,), (1,)), ((), ())), preferred_element_type=F32)


def kernel(
    tiles,
    psi_in,
    pot_in,
    projector_in,
    coupling_in,
    slot_live,
    point_count_in,
    point_index_in,
    out,
    gram,
    psi,
    pot,
    projector,
    coupling,
    point_count,
    point_index,
    field,
    low_x,
    high_x,
    other_y,
    other_band,
    hot,
    lot_of,
    lot_of16,
    row_of,
    lane_of,
    operator,
    parts,
    added,
    given,
    local,
    wide,
    wide_other,
    send,
    recv,
    send_band,
    recv_band,
    sums,
    sums_in,
    send_sums,
    recv_sums,
    load,
):
    groups = field.shape[1]
    band = lax.axis_index("band")
    tile = lax.axis_index("space")
    up = (band, lax.rem(tile + 2, tiles))
    down = (band, lax.rem(tile + tiles - 2, tiles))
    beside = (band, tile + 1 - 2 * lax.rem(tile, 2))
    across = (1 - band, tile)

    def turned_by(span, low, away):
        return (band, tile - lax.rem(tile, span) + lax.rem(lax.rem(tile, span) + away * low, span))

    depth = tiles // 32
    ring = band * depth + tile // 32

    def along(away):
        place = lax.rem(ring + away, 2 * depth)
        return (place // depth, lax.rem(place, depth) * 32 + lax.rem(tile, 32))

    phases = (
        [beside],
        [turned_by(32, 2, away) for away in range(1, 16)],
        [along(away) for away in range(1, 2 * depth)],
    )

    def loaded(src, dst, at):
        return pltpu.make_async_copy(src, dst, load.at[at])

    loads = [
        loaded(psi_in.at[pl.ds(g * GB, GB)], psi.at[pl.ds(g * GB, GB)], g) for g in range(groups)
    ] + [
        loaded(src, dst, groups + at)
        for at, (src, dst) in enumerate(
            (
                (point_index_in, point_index),
                (projector_in, projector),
                (coupling_in, coupling),
                (point_count_in, point_count),
                (pot_in, pot),
            )
        )
    ]
    for copy in loads[:groups]:
        copy.start()

    greeted = [device for phase in phases[::-1] for device in phase] + [up, down]
    barrier = pltpu.get_barrier_semaphore()
    for device in greeted:
        pl.semaphore_signal(barrier, inc=1, device_id=device, device_id_type=MESH)
    for copy in loads[groups:]:
        copy.start()

    def halo_copies(turn, g):
        def copy(src, dst, which, device):
            return pltpu.make_async_remote_copy(
                src_ref=src,
                dst_ref=dst,
                send_sem=send.at[turn, g, which],
                recv_sem=recv.at[turn, g, which],
                device_id=device,
                device_id_type=MESH,
            )

        block = field.at[turn, g]
        copies = []
        for half in range(2):
            rows = pl.ds(half * LOT, LOT)
            copies += [
                copy(
                    block.at[pl.ds(SX - WIDTH, WIDTH), rows],
                    low_x.at[turn, g, :, rows],
                    2 * half,
                    up,
                ),
                copy(block.at[pl.ds(0, WIDTH), rows], high_x.at[turn, g, :, rows], 2 * half + 1, down),
            ]
        return copies + [copy(block, other_y.at[turn, g], 4, beside)]

    def band_copy(g, half):
        rows = pl.ds(half * LOT, LOT)
        return pltpu.make_async_remote_copy(
            src_ref=field.at[0, g, pl.ds(band * (SX // 2), SX // 2), rows],
            dst_ref=other_band.at[g, :, rows],
            send_sem=send_band.at[g, half],
            recv_sem=recv_band.at[g, half],
            device_id=across,
            device_id_type=MESH,
        )

    def split_lot(g, lot, rows):
        parts[g, lot] = two_parts(jnp.concatenate(rows, axis=1))

    for g in range(groups):
        loads[g].wait()
        for b in range(GB):
            for x in range(SX):
                field[0, g, x, :, b, :] = psi[g * GB + b, pl.ds(x * SY, SY)]
        if g == 0:
            pl.semaphore_wait(barrier, len(greeted))
        for copy in halo_copies(0, g):
            copy.start()

    field[1] = jnp.zeros(field.shape[1:], F32)
    for copy in loads[groups:]:
        copy.wait()

    @pl.loop(0, SLOTS, unroll=8)
    def _(s):
        cols = pl.ds(pl.multiple_of(s * PTS, PTS), PTS)
        index = point_index[pl.ds(s, 1), :]
        place = jnp.broadcast_to(index & (PLACES - 1), (PLACES, PTS))
        spots = lax.broadcasted_iota(jnp.int32, (PLACES, PTS), 0)
        hot[:, cols] = jnp.where(place == spots, 1.0, 0.0).astype(BF16)
        row_of[:, cols] = jnp.broadcast_to(index // SZ, (GB, PTS))
        lane_of[:, cols] = jnp.broadcast_to(index & (SZ - 1), (GB, PTS))
        lot = jnp.broadcast_to(index // PLACES, (16, PTS))
        lot_of[:, cols] = lot
        lot_of16[:, cols] = lot.astype(F32).astype(BF16)
        points = lax.broadcasted_iota(jnp.int32, (NPROJ, PTS), 1)
        slots = jnp.full((NPROJ, PTS), s, jnp.int32)
        keep = (points < point_count[s]) & (slots < slot_live[0])
        weights = jnp.where(keep, projector[s], 0.0)
        mine = lax.broadcasted_iota(jnp.int32, (NPROJ, SLOTS), 1) == s
        couple = jnp.sum(jnp.where(mine, coupling[...], 0.0), axis=1, keepdims=True)
        coupled = weights * couple
        weights_high = weights.astype(BF16).astype(F32)
        coupled_high = coupled.astype(BF16).astype(F32)
        left = jnp.concatenate([weights_high, weights_high, weights - weights_high], axis=0)
        right = jnp.concatenate([coupled_high, coupled - coupled_high, coupled_high], axis=0)
        square = dot(left.T.astype(BF16), right.astype(BF16))
        square_high = square.astype(BF16).astype(F32)
        operator[s] = jnp.concatenate([square_high, square - square_high], axis=1).astype(BF16)

    def gathered(g, piece):
        cols = pl.ds(piece * CHUNK, CHUNK)
        picked = dot(parts[g].reshape(LOTS * 16, PLACES), hot[:, cols])
        lots = lot_of[:, cols]
        values = jnp.zeros((16, CHUNK), F32)
        for lot in range(LOTS):
            values = jnp.where(lots == lot, picked[16 * lot : 16 * lot + 16], values)
        return values[:8] + values[8:]

    def gathered_by_lanes(turn, g, piece):
        values = []
        for s in range(CHUNK // PTS):
            cols = pl.ds(piece * CHUNK + s * PTS, PTS)
            lanes, rows = lane_of[:, cols], row_of[:, cols]
            found = jnp.zeros((GB, PTS), F32)
            for row in range(ROWS):
                picked = jnp.take_along_axis(
                    field[turn, g, row // SY, row % SY], lanes, axis=1, mode="promise_in_bounds"
                )
                found = jnp.where(rows == row, picked, found)
            values.append(found)
        return jnp.concatenate(values, axis=1)

    def operated(values, piece):
        given = []
        nothing = jnp.zeros((16, PTS), BF16)
        for s in range(0, CHUNK // PTS, 2):
            first = two_parts(values[:, s * PTS : (s + 1) * PTS])
            second = two_parts(values[:, (s + 1) * PTS : (s + 2) * PTS])
            both = jnp.concatenate(
                [
                    jnp.concatenate([first, nothing], axis=1),
                    jnp.concatenate([nothing, second], axis=1),
                ],
                axis=0,
            )
            at = piece * (CHUNK // PTS) + s
            products = dot(both, operator[at : at + 2].reshape(2 * PTS, 2 * PTS))
            for product in (products[:16], products[16:]):
                given.append(
                    two_parts(product[:8, :PTS] + (product[:8, PTS:] + product[8:, :PTS]))
                )
        return jnp.concatenate(given, axis=1)

    def gather_and_operate(turn, g):
        values = [
            gathered_by_lanes(turn, g, piece) if piece in LANE_PIECES else gathered(g, piece)
            for piece in range(PIECES)
        ]
        for piece in range(PIECES):
            given[:, piece * CHUNK : (piece + 1) * CHUNK] = operated(values[piece], piece)

    def scatter(g):
        amounts = given[...]
        lots = lot_of16[...]
        nothing = jnp.zeros_like(amounts)
        spread = [jnp.where(lots == lot, amounts, nothing) for lot in range(LOTS)]
        added[g] = dot_t(jnp.concatenate(spread, axis=0), hot[...])

    def stencil_plane(turn, g, x, diagonal):
        own = [field[turn, g, x, y] for y in range(SY)]
        ring = own + [other_y[turn, g, x, y] for y in range(SY)]
        for y in range(SY):
            value = own[y]
            total = value * (jnp.broadcast_to(pot[pl.ds(x * SY + y, 1)], (GB, SZ)) + diagonal)
            for k in range(1, WIDTH + 1):
                near = ring[(y + k) % (2 * SY)] + ring[(y - k) % (2 * SY)]
                near += pltpu.roll(value, k, axis=1) + pltpu.roll(value, SZ - k, axis=1)
                if x - k >= 0:
                    near += field[turn, g, x - k, y]
                if x + k < SX:
                    near += field[turn, g, x + k, y]
                total += (KINETIC * LAP_COEFFS[k]) * near
            local[g, x, y] = total

    def finish(step, turn, g, half):
        for copy in halo_copies(turn, g)[2 * half : 2 * half + 2]:
            copy.wait()
        scale, carry = chosen(step, SCALE), chosen(step, CARRY)
        for x in range(SX):
            lot = x * (SY // LOT) + half
            spread = added[g, pl.ds(16 * lot, 16)]
            spread = spread[:8] + spread[8:]
            new = []
            for e in range(LOT):
                y = half * LOT + e
                total = local[g, x, y] + spread[:, e * SZ : (e + 1) * SZ]
                for j in range(WIDTH):
                    if j >= x:
                        total += (KINETIC * LAP_COEFFS[x + WIDTH - j]) * low_x[turn, g, j, y]
                    if j <= x - 2:
                        total += (KINETIC * LAP_COEFFS[SX + j - x]) * high_x[turn, g, j, y]
                value = scale * total + carry * field[1 - turn, g, x, y]
                field[1 - turn, g, x, y] = value
                new.append(value)
            split_lot(g, lot, new)

        @pl.when(step < STEPS - 1)
        def _():
            following = halo_copies(1 - turn, g)
            for copy in following[2 * half : 2 * half + 2] + following[4:] * half:
                copy.start()

        @pl.when(step == STEPS - 1)
        def _():
            band_copy(g, half).start()

    for g in range(groups):
        for lot in range(LOTS):
            x, half = lot // (SY // LOT), lot % (SY // LOT)
            split_lot(g, lot, [field[0, g, x, half * LOT + e] for e in range(LOT)])

    rounds = STEPS * groups

    def place_of(at):
        step = at // groups
        return step, step % 2, at % groups

    @pl.loop(0, rounds)
    def _(at):
        step, turn, g = place_of(at)
        before = place_of(lax.rem(at + rounds - 1, rounds))
        gather_and_operate(turn, g)

        @pl.when(at > 0)
        def _():
            finish(*before, 0)

        halo_copies(turn, g)[4].wait()
        scatter(g)
        diagonal = 3.0 * KINETIC * LAP_COEFFS[0] - chosen(step, SHIFT)
        for x in range(SX):
            stencil_plane(turn, g, x, diagonal)

        @pl.when(at > 0)
        def _():
            finish(*before, 1)

    finish(*place_of(rounds - 1), 0)
    finish(*place_of(rounds - 1), 1)

    bands = groups * GB
    for g in range(groups):
        for b in range(GB):
            for x in range(SX):
                out[g * GB + b, pl.ds(x * SY, SY)] = field[0, g, x, :, b, :]
    quarter = ROWS // 4

    def quarter_rows():
        return [(x, y) for x in range(SX // 2) for y in range(LOT)]

    for at in range(4):
        for n, (x, y) in enumerate(quarter_rows()):
            x, y = x + at // 2 * (SX // 2), y + at % 2 * LOT
            row = at * quarter + n
            wide[:, row * SZ : (row + 1) * SZ] = two_parts(
                jnp.concatenate([field[0, g, x, y] for g in range(groups)], axis=0)
            )

    def folded(product):
        rows, cols = product.shape[0] // 2, product.shape[1] // 2
        return (product[:rows, :cols] + product[rows:, cols:]) + (
            product[:rows, cols:] + product[rows:, :cols]
        )

    def keep_term(term, row, col):
        for at in range(0, term.shape[0], GB):
            lane = (row + at) // GB * 64 + col
            sums[0, :, lane : lane + term.shape[1]] = term[at : at + GB]

    def kept_term(sum_, col):
        return jnp.concatenate([sum_[:, col : col + bands], sum_[:, 64 + col : 64 + col + bands]], axis=0)

    sums[0] = jnp.zeros(sums.shape[1:], F32)
    block = wide[...]
    keep_term(folded(dot_t(block, block)), 0, 0)

    depth_of = quarter * SZ
    for g in range(groups):
        term = None
        for half in range(2):
            start = (2 * (1 - band) + half) * depth_of
            kept = wide[:, pl.ds(pl.multiple_of(start, depth_of), depth_of)]
            band_copy(g, half).wait()
            for n, (x, y) in enumerate(quarter_rows()):
                wide_other[:, n * SZ : (n + 1) * SZ] = two_parts(
                    other_band[g, x, half * LOT + y]
                )
            part = dot_t(kept, wide_other[...])
            term = part if term is None else term + part
        keep_term(folded(term), 0, bands + g * GB)

    used = 0
    for at, phase in enumerate(phases):
        copies = []
        for device in phase:
            copies.append(
                pltpu.make_async_remote_copy(
                    src_ref=sums.at[at],
                    dst_ref=sums_in.at[used],
                    send_sem=send_sums.at[used],
                    recv_sem=recv_sums.at[used],
                    device_id=device,
                    device_id_type=MESH,
                )
            )
            copies[-1].start()
            used += 1
        for copy in copies:
            copy.wait()
        total = sums[at]
        if at + 1 < len(phases):
            for n in range(len(phase)):
                total += sums_in[used - len(phase) + n]
            sums[at + 1] = total

    other = jnp.zeros_like(total)
    for n in range(len(phases[-1])):
        came = sums_in[used - len(phases[-1]) + n]
        place = lax.rem(ring + 2 * depth - (n + 1), 2 * depth)
        same = jnp.full(came.shape, place // depth, jnp.int32) == band
        total += jnp.where(same, came, 0.0)
        other += jnp.where(same, 0.0, came)
    own = kept_term(total, 0)
    mixed = kept_term(total, bands) + kept_term(other, bands).T
    first = jnp.full(own.shape, band, jnp.int32) == 0
    weight = 1.0 / (tiles * ROWS * SZ)
    gram[:, :bands] = jnp.where(first, own, mixed) * weight
    gram[:, bands:] = jnp.where(first, mixed, own) * weight


def in_hbm(array):
    return pltpu.with_memory_space_constraint(array, pltpu.HBM)


def per_device(tiles, psi, potential, projector, coupling, slot_live, point_count, point_index):
    bands = psi.shape[0]
    groups = bands // GB
    hbm = pl.BlockSpec(memory_space=pltpu.HBM)
    vmem = pl.BlockSpec(memory_space=pltpu.VMEM)
    smem = pl.BlockSpec(memory_space=pltpu.SMEM)
    filtered, gram = pl.pallas_call(
        functools.partial(kernel, tiles),
        out_shape=(
            jax.ShapeDtypeStruct((bands, ROWS, SZ), F32),
            jax.ShapeDtypeStruct((bands, 2 * bands), F32),
        ),
        in_specs=[hbm] * 4 + [smem] + [hbm] * 2,
        out_specs=(vmem, vmem),
        scratch_shapes=[
            pltpu.VMEM((bands, ROWS, SZ), F32),
            pltpu.VMEM((ROWS, SZ), F32),
            pltpu.VMEM((SLOTS, NPROJ, PTS), F32),
            pltpu.VMEM((NPROJ, SLOTS), F32),
            pltpu.SMEM((SLOTS,), jnp.int32),
            pltpu.VMEM((SLOTS, PTS), jnp.int32),
            pltpu.VMEM((2, groups, SX, SY, GB, SZ), F32),
            pltpu.VMEM((2, groups, WIDTH, SY, GB, SZ), F32),
            pltpu.VMEM((2, groups, WIDTH, SY, GB, SZ), F32),
            pltpu.VMEM((2, groups, SX, SY, GB, SZ), F32),
            pltpu.VMEM((groups, SX // 2, SY, GB, SZ), F32),
            pltpu.VMEM((PLACES, POINTS), BF16),
            pltpu.VMEM((16, POINTS), jnp.int32),
            pltpu.VMEM((16, POINTS), BF16),
            pltpu.VMEM((GB, POINTS), jnp.int32),
            pltpu.VMEM((GB, POINTS), jnp.int32),
            pltpu.VMEM((SLOTS, PTS, 2 * PTS), BF16),
            pltpu.VMEM((groups, LOTS, 16, PLACES), BF16),
            pltpu.VMEM((groups, LOTS * 16, PLACES), F32),
            pltpu.VMEM((16, POINTS), BF16),
            pltpu.VMEM((groups, SX, SY, GB, SZ), F32),
            pltpu.VMEM((2 * bands, ROWS * SZ), BF16),
            pltpu.VMEM((2 * GB, ROWS * SZ // 4), BF16),
            pltpu.SemaphoreType.DMA((2, groups, 5)),
            pltpu.SemaphoreType.DMA((2, groups, 5)),
            pltpu.SemaphoreType.DMA((groups, 2)),
            pltpu.SemaphoreType.DMA((groups, 2)),
            pltpu.VMEM((3, GB, 128), F32),
            pltpu.VMEM((23, GB, 128), F32),
            pltpu.SemaphoreType.DMA((23,)),
            pltpu.SemaphoreType.DMA((23,)),
            pltpu.SemaphoreType.DMA((groups + 6,)),
        ],
        compiler_params=pltpu.CompilerParams(
            collective_id=0, has_side_effects=True, vmem_limit_bytes=40 << 20
        ),
        name="filter",
    )(
        in_hbm(psi.reshape(bands, ROWS, SZ)),
        in_hbm(potential.reshape(ROWS, SZ)),
        in_hbm(projector[0]),
        in_hbm(jnp.swapaxes(coupling, 1, 2)[0]),
        slot_live,
        in_hbm(point_count[0]),
        in_hbm(point_index[0]),
    )
    return filtered.reshape(psi.shape), gram


def solution(mesh):
    placed = (
        P("band", "space", None, None, None),
        P("space", None, None, None),
        P("space", None, None, None),
        P("space", None, None),
        P("space"),
        P("space", None),
        P("space", None, None),
    )
    return jax.shard_map(
        functools.partial(per_device, mesh.shape["space"]),
        mesh=mesh,
        in_specs=placed,
        out_specs=(P("band", "space", None, None, None), P("band", None)),
        check_vma=False,
    )
```
